256 devices in a mesh: ctx: 32 (over y, z), head: 8 (over x, core).
Axes of the slice: x: 4, y: 4, z: 8, core: 2. Of those that a mesh axis runs over, the one named last changes fastest.
Arguments:
- queries: bfloat16 [8, 16384, 128], P('head', 'ctx'), may hold values from -170 to 170
- keys: bfloat16 [16384, 128], P('ctx'), may hold values from -6 to 6
- values: bfloat16 [16384, 128], P('ctx'), may hold values from -6 to 6
- outputs: bfloat16 [8, 16384, 128], P('head', 'ctx'), may hold values from -2 to 2
- dout: bfloat16 [8, 16384, 128], P('head', 'ctx'), may hold values from -6 to 6
- docs: int32 [16384], P('ctx'), may hold values from 0 to 63, never falling along the last dimension, each value on 1 to 8704 neighbouring positions
Outputs:
- dq: bfloat16 [8, 16384, 128], P('head', 'ctx')
- dk: bfloat16 [16384, 128], P(('ctx', 'head'))
- dv: bfloat16 [16384, 128], P(('ctx', 'head'))
The draws below stay inside these ranges and needn't reach their ends.
Inputs may be any that keep to these rules, and one draw needn't show every extreme that they name: `docs`: document numbers never fall along the sequence; each document holds 1 to 8704 tokens and one holds exactly 8704.
All inputs are finite; a program needn't handle non-finite values.
Results may differ from the reference program's by a relative error of at most 0.0049.
Values may be sent and summed in bfloat16 or wider, within the bound.
No kernel may reach another device: no remote copies, remote signals or barrier semaphores. Data moves between devices by JAX's collectives and lax.ppermute only.
A program may use at most 64 MiB of HBM per device.

```python
import math
import jax
import jax.numpy as jnp
import numpy as np
from jax import lax

HD = 128
HEADS = 8
TOKENS = 16384
DOC_MOST = 8704
DOCS = 64


def drawn_rows(key):
    base = jnp.clip(jax.random.normal(key, (TOKENS, HD), jnp.float32), -6.0, 6.0)
    return base


def draw_keys(key, part):
    base = drawn_rows(key)
    return base.astype(jnp.bfloat16)


def draw_queries(key, part):
    key = jax.random.fold_in(key, 9)
    fresh = jnp.clip(jax.random.normal(key, (HEADS, TOKENS, HD), jnp.float32), -6.0, 6.0)
    return fresh.astype(jnp.bfloat16)


def level_of(stream_key, dims, pieces, least, top_value):
    factor_of = 1.0
    for dim, parts in pieces:
        heights = jax.random.uniform(jax.random.fold_in(jax.random.fold_in(stream_key, 6), dim), (parts,), jnp.float32, least / len(pieces), top_value / len(pieces))
        factor_of = factor_of * jnp.repeat(jnp.exp(heights), dims[dim] // parts).reshape((-1,) + (1,) * (len(dims) - 1 - dim))
    return factor_of


def split_up(number_of, total, reach, skew):
    loads = [(1 << 20) // math.isqrt(rank ** skew) + 1 for rank in range(2, number_of + 1)]
    surplus, holding = total - reach - (number_of - 1), [1] * (number_of - 1)
    while surplus > 0:
        movable = [i for i in range(number_of - 1) if holding[i] < reach]
        pool, left = sum([loads[i] for i in movable]), surplus
        for i in movable:
            addition = min(reach - holding[i], max(1, left * loads[i] // pool), surplus)
            holding[i] = holding[i] + addition
            surplus = surplus - addition
    return np.array([reach] + holding)


def ragged(own_key, number_of, total, most, skew):
    if number_of == 2:
        one = jax.random.randint(own_key, (), max(1, total - most), min(most, total - 1) + 1)
        return jnp.stack([one, total - one])
    sizes = jnp.asarray(split_up(number_of, total, most, skew), jnp.int32)
    couples = (number_of - 1) // 2
    donor, receiver = sizes[1:1 + 2 * couples:2], sizes[2:2 + 2 * couples:2]
    room = jnp.minimum(donor - 1, most - receiver)
    passed = jax.random.randint(jax.random.fold_in(own_key, 1), (couples,), 0, 1 << 20) % (room + 1)
    sizes = sizes.at[1:1 + 2 * couples:2].set(donor - passed).at[2:2 + 2 * couples:2].set(receiver + passed)
    return sizes[jax.random.permutation(jax.random.fold_in(own_key, 2), number_of)]


def noise(rng, extent, width, limit, split=(), kind=jnp.bfloat16):
    entries = jax.random.normal(rng, extent, jnp.float32) * width
    if len(split) > 0:
        entries = level_of(rng, extent, split, -0.22, 0.18) * entries
    return jnp.clip(entries, min=-limit, max=limit).astype(kind)


def setup_inputs(seed: int = 0) -> dict:
    seeds = jax.random.split(jax.random.key(seed), 7)
    return {
        "queries": draw_queries(jax.random.fold_in(seeds[6], 71), 0),
        "keys": draw_keys(jax.random.fold_in(seeds[6], 71), 0),
        "values": noise(seeds[2], (TOKENS, HD), 1.0, 6.0, ((0, 32),)),
        "outputs": noise(seeds[3], (HEADS, TOKENS, HD), 0.3, 2.0, ((0, 8), (1, 32))),
        "dout": noise(seeds[4], (HEADS, TOKENS, HD), 1.0, 6.0, ((0, 8), (1, 32))),
        "docs": jnp.searchsorted(jnp.cumsum(ragged(seeds[5], DOCS, TOKENS, DOC_MOST, 1)), jnp.arange(TOKENS), side="right").astype(jnp.int32),
    }


def reference(queries, keys, values, outputs, dout, docs):
    scale = 1.0 / (HD ** 0.5)
    qblock = min(1024, TOKENS)
    nq = TOKENS // qblock
    window = min(TOKENS, DOC_MOST + qblock)
    delta_all = jnp.sum(dout.astype(jnp.float32) * outputs.astype(jnp.float32), axis=-1)

    def block(carry, index):
        dk_acc, dv_acc = carry
        head_id = (index // nq).astype(jnp.int32)
        qstart = ((index % nq) * qblock).astype(jnp.int32)
        wstart = jnp.clip(qstart + qblock - window, 0, TOKENS - window).astype(jnp.int32)
        query = lax.dynamic_slice_in_dim(lax.dynamic_index_in_dim(queries, head_id, 0, keepdims=False), qstart, qblock, 0)
        grad_out = lax.dynamic_slice_in_dim(lax.dynamic_index_in_dim(dout, head_id, 0, keepdims=False), qstart, qblock, 0)
        delta = lax.dynamic_slice_in_dim(lax.dynamic_index_in_dim(delta_all, head_id, 0, keepdims=False), qstart, qblock, 0)
        key_blk = lax.dynamic_slice_in_dim(keys, wstart, window, 0)
        val_blk = lax.dynamic_slice_in_dim(values, wstart, window, 0)
        qdoc = lax.dynamic_slice_in_dim(docs, qstart, qblock, 0)
        kdoc = lax.dynamic_slice_in_dim(docs, wstart, window, 0)
        qpos = qstart + jnp.arange(qblock, dtype=jnp.int32)
        kpos = wstart + jnp.arange(window, dtype=jnp.int32)
        visible = (qdoc[:, None] == kdoc[None, :]) & (kpos[None, :] <= qpos[:, None])
        score = jnp.dot(query, key_blk.T, preferred_element_type=jnp.float32) * scale
        score = jnp.where(visible, score, jnp.float32(-1e30))
        top = jnp.max(score, axis=1)
        total = jnp.sum(jnp.where(visible, jnp.exp(score - top[:, None]), jnp.float32(0.0)), axis=1)
        lse = top + jnp.log(total)
        prob = jnp.where(visible, jnp.exp(score - lse[:, None]), jnp.float32(0.0))
        dprob = jnp.dot(grad_out, val_blk.T, preferred_element_type=jnp.float32)
        dscore = (prob * (dprob - delta[:, None])).astype(jnp.bfloat16)
        dq_blk = (jnp.dot(dscore, key_blk, preferred_element_type=jnp.float32) * scale).astype(jnp.bfloat16)
        dv_t = jnp.dot(prob.astype(jnp.bfloat16).T, grad_out, preferred_element_type=jnp.float32)
        dk_t = jnp.dot(dscore.T, query, preferred_element_type=jnp.float32) * scale
        dk_acc = lax.dynamic_update_slice_in_dim(dk_acc, lax.dynamic_slice_in_dim(dk_acc, wstart, window, 0) + dk_t, wstart, 0)
        dv_acc = lax.dynamic_update_slice_in_dim(dv_acc, lax.dynamic_slice_in_dim(dv_acc, wstart, window, 0) + dv_t, wstart, 0)
        return (dk_acc, dv_acc), dq_blk

    zeros = jnp.zeros((TOKENS, HD), jnp.float32)
    (dk_acc, dv_acc), dq_blocks = lax.scan(block, (zeros, zeros), jnp.arange(HEADS * nq, dtype=jnp.int32))
    dq = dq_blocks.reshape(HEADS, TOKENS, HD)
    return dq, dk_acc.astype(jnp.bfloat16), dv_acc.astype(jnp.bfloat16)
```

```python
import functools
import math

import jax
import jax.numpy as jnp
from jax import lax
from jax.experimental import pallas as pl
from jax.experimental.pallas import tpu as pltpu
from jax.sharding import Mesh
from jax.sharding import PartitionSpec as P

BF16 = jnp.bfloat16
F32 = jnp.float32
NY, NX, NC = 4, 4, 2
DOCS = 64
EXTRA = 16
LOW = -1e30
TILE = 256
LOG2E = 1.0 / math.log(2.0)


def dot(left, right, left_dim, right_dim):
    return lax.dot_general(
        left, right, (((left_dim,), (right_dim,)), ((), ())), preferred_element_type=F32
    )


def split_row(row, count):
    part = row.shape[1] // count
    return [row[:, i * part : (i + 1) * part] for i in range(count)]


def rows_to_line(block):
    return jnp.concatenate([block[i : i + 1] for i in range(block.shape[0])], axis=1)


def prep_kernel(place, q, do, out, keys, values, docs, sent, pieces):
    tok, width = q.shape
    at = tok + EXTRA
    docs_rows = jnp.concatenate(split_row(docs[...].astype(F32), tok // width), axis=0)
    sent[0:tok, :] = q[...]
    pad = jnp.zeros((EXTRA - docs_rows.shape[0], width), F32)
    sent[tok:at, :] = jnp.concatenate([docs_rows, pad], axis=0).astype(BF16)
    prod = do[...].astype(F32) * out[...].astype(F32)
    delta = jnp.sum(jnp.transpose(prod), axis=0, keepdims=True)
    rows = jnp.concatenate(split_row(delta, tok // width), axis=0)
    high = rows.astype(BF16).astype(F32)
    middle = (rows - high).astype(BF16).astype(F32)
    low = rows - high - middle
    pad = jnp.zeros((EXTRA - 3 * rows.shape[0], width), F32)
    sent[at : at + tok, :] = do[...]
    sent[at + tok : 2 * at, :] = jnp.concatenate([high, middle, low, pad], axis=0).astype(BF16)
    share = (pieces.shape[1] - EXTRA) // 2
    first = pl.multiple_of(place[0] * share, share)
    line = lax.broadcasted_iota(jnp.int32, docs_rows.shape, 0)
    mine = jnp.sum(jnp.where(line == place[0] // NC, docs_rows, 0.0), axis=0, keepdims=True)
    line = lax.broadcasted_iota(jnp.int32, (EXTRA, width), 0)
    extra = jnp.where(line == 0, mine, 0.0).astype(BF16)
    key_rows, value_rows = keys[pl.ds(first, share), :], values[pl.ds(first, share), :]
    for i in range(pieces.shape[0]):
        pieces[i, 0:share, :] = key_rows
        pieces[i, share : share + EXTRA, :] = extra
        pieces[i, share + EXTRA :, :] = value_rows


def high_kernel(share, nz, place, rows, ends):
    x, y, z = place[1], place[2], place[3]
    tok = rows.shape[2]
    line = lax.broadcasted_iota(jnp.int32, (1, tok), 1)
    for m in range(NX):
        before, skipped = (lax.rem(y + x - m + NX, NY) * nz + z) * share, place[0] * share
        rows[m] = (before + jnp.clip(line - skipped + 1, 0, share)).astype(F32)
        ends[m, 0] = before + jnp.clip(1 - skipped, 0, share)
        ends[m, 1] = before + jnp.clip(tok - skipped, 0, share)


def tile_loops(bounds, m, step, carry):
    first = bounds[m, 0] // TILE
    last = (bounds[m, 3] + TILE - 1) // TILE
    full_first = jnp.minimum((bounds[m, 1] + TILE - 1) // TILE, last)
    full_last = jnp.maximum(bounds[m, 2] // TILE, full_first)
    carry = lax.fori_loop(first, full_first, functools.partial(step, True), carry)
    carry = lax.fori_loop(full_first, full_last, functools.partial(step, False), carry)
    return lax.fori_loop(full_last, last, functools.partial(step, True), carry)


def visible_of(tile, tok, low, high):
    index = (lax.broadcasted_iota(jnp.int32, (TILE, tok), 0) + tile * TILE).astype(F32)
    return (index >= low) & (index < high)


def stats_kernel(factor, place, ends, own, peer, high_in, p0, p1, p2, p3, lse, key_all, low_out, bounds):
    x, y, c = place[1], place[2], place[4]
    nz, rows, width = p2.shape
    share = rows - EXTRA
    tok = own.shape[1] // 2 - EXTRA
    number = lax.broadcasted_iota(jnp.int32, (DOCS, width), 0).astype(F32)
    below = jnp.zeros((DOCS, width), F32)
    for k, piece in enumerate((p0, p1, p2, p3)):
        for i in range(nz):
            where = block_row(y, k, i, nz, share)
            key_all[pl.ds(where, share), :] = piece[i, 0:share, :]
            docs = piece[i, share : share + EXTRA, :].astype(F32)[0:1, :]
            below = below + jnp.where(docs < number, 1.0, 0.0)
    lane = lax.broadcasted_iota(jnp.int32, (DOCS, width), 1)
    ours = (lane >= c * share) & (lane < (c + 1) * share)
    below = jnp.sum(jnp.where(ours, below, 0.0), axis=1, keepdims=True)
    number = lax.broadcasted_iota(jnp.int32, (DOCS, tok), 0).astype(F32)
    for m in range(NY):
        docs = rows_to_line(own[m, tok : tok + EXTRA, :].astype(F32)[0 : tok // width])
        low = jnp.sum(jnp.where(docs == number, below, 0.0), axis=0, keepdims=True)
        low_out[m] = low
        bounds[m, 0] = jnp.min(low).astype(jnp.int32)
        bounds[m, 1] = jnp.max(low).astype(jnp.int32)
        bounds[m, 2] = ends[m, 0]
        bounds[m, 3] = ends[m, 1]

    def group(m, carry):
        low = low_out[m]
        high = high_in[m]
        pair = [sets[m, 0:tok, :] for sets in (own, peer)]

        def step(masked, tile, state):
            key = key_all[pl.ds(pl.multiple_of(tile * TILE, TILE), TILE), :]
            visible = visible_of(tile, tok, low, high) if masked else None
            after = []
            for query, (top, total) in zip(pair, state):
                score = dot(key, query, 1, 1) * factor
                if masked:
                    score = jnp.where(visible, score, LOW)
                new_top = jnp.maximum(top, jnp.max(score, axis=0, keepdims=True))
                terms = jnp.sum(jnp.exp2(score - new_top), axis=0, keepdims=True)
                after.append((new_top, total * jnp.exp2(top - new_top) + terms))
            return tuple(after)

        start = (jnp.full((1, tok), LOW, F32), jnp.zeros((1, tok), F32))
        for half, (top, total) in enumerate(tile_loops(bounds, m, step, (start,) * NC)):
            lse[NC * lax.rem(x - m + NX, NX) + (NC - 1 - c if half else c)] = jnp.where(top > LOW, top + jnp.log2(jnp.maximum(total, 1e-30)), LOW)
        return carry

    lax.fori_loop(0, NY, group, 0)


def join(*parts):
    top = functools.reduce(jnp.maximum, parts)
    return top + jnp.log2(sum(jnp.exp2(part - top) for part in parts))


def grad_kernel(
    factor, scale, place, bounds, own, peer, high_in, p0, p1, p2, p3, key_all, low_in, l0, l1, l2, l3,
    dq_own, dq_peer, here, up, down, far_dk, far_dv, value_all, dk, dv, lse, dq_turned,
):
    x, y, c = place[1], place[2], place[4]
    nz, share, width = p2.shape
    slab = nz * share
    tok = own.shape[1] // 2 - EXTRA
    for k, piece in enumerate((p0, p1, p2, p3)):
        for i in range(nz):
            where = block_row(y, k, i, nz, share)
            value_all[pl.ds(where, share), :] = piece[i, piece.shape[1] - share :, :]
    dk[...] = jnp.zeros_like(dk)
    dv[...] = jnp.zeros_like(dv)
    lse[...] = join(l0[...], l1[...], l2[...], l3[...])
    n = tok // width

    def group(m, carry):
        low = low_in[m]
        high = high_in[m]
        heads = []
        for sets, head in ((own, c), (peer, NC - 1 - c)):
            at = tok + EXTRA
            extra = sets[m, at + tok : 2 * at, :].astype(F32)
            delta = rows_to_line(extra[0:n] + extra[n : 2 * n] + extra[2 * n : 3 * n])
            heads.append((sets[m, 0:tok, :], sets[m, at : at + tok, :], delta, lse[NC * lax.rem(x - m + NX, NX) + head]))
        dq_turned[...] = jnp.zeros_like(dq_turned)

        def step(masked, tile, carry):
            at = pl.ds(pl.multiple_of(tile * TILE, TILE), TILE)
            key, value = key_all[at, :], value_all[at, :]
            visible = visible_of(tile, tok, low, high) if masked else None
            new_dk, new_dv = dk[at, :], dv[at, :]
            for half, (query, grad, delta, norm) in enumerate(heads):
                prob = jnp.exp2(dot(key, query, 1, 1) * factor - norm)
                if masked:
                    prob = jnp.where(visible, prob, 0.0)
                dprob = dot(value, grad, 1, 1)
                dscore = (prob * (dprob - delta)).astype(BF16)
                new_dv = new_dv + dot(prob.astype(BF16), grad, 1, 0)
                new_dk = new_dk + dot(dscore, query, 1, 0)
                dq_turned[half] += dot(key, dscore, 0, 0)
            dk[at, :] = new_dk
            dv[at, :] = new_dv
            return carry

        tile_loops(bounds, m, step, 0)
        dq_own[m] = jnp.transpose(dq_turned[0]) * scale
        dq_peer[m] = jnp.transpose(dq_turned[1]) * scale
        return carry

    lax.fori_loop(0, NY, group, 0)

    def slab_of(ref, by):
        at = pl.ds(pl.multiple_of(lax.rem(y + by, NY) * slab, slab), slab)
        return (ref[at, :] * (scale if ref is dk else 1.0)).astype(BF16).reshape(nz, share, width)

    for out, by in ((here, 0), (up, 1), (down, NY - 1)):
        out[:, 0] = slab_of(dk, by)
        out[:, 1] = slab_of(dv, by)
    far_dk[...] = slab_of(dk, 2)
    far_dv[...] = slab_of(dv, 2)


def block_row(y, k, i, nz, share):
    return pl.multiple_of((lax.rem(y - k + NY, NY) * nz + i) * share, share)


def query_kernel(own, there, *outs):
    for k, out in enumerate(outs):
        out[...] = (own[k] + there[k]).astype(BF16)


def stack_kernel(*refs):
    for i, piece in enumerate(refs[:-1]):
        refs[-1][i] = piece[...]


def add_kernel(*refs):
    total = refs[0][...].astype(F32)
    for ref in refs[1:-1]:
        total = total + ref[...].astype(F32)
    refs[-1][...] = total.astype(BF16)


def relay_kernel(up, down, got_dk, got_dv, new_up, new_down):
    new_up[:, 0] = (up[:, 0].astype(F32) + got_dk[...].astype(F32)).astype(BF16)
    new_up[:, 1] = up[:, 1]
    new_down[:, 0] = down[:, 0]
    new_down[:, 1] = (down[:, 1].astype(F32) + got_dv[...].astype(F32)).astype(BF16)


def last_kernel(blocks, dk, dv):
    total = blocks[0].astype(F32)
    for i in range(1, blocks.shape[0]):
        total = total + blocks[i].astype(F32)
    dk[...] = total[0].astype(BF16)
    dv[...] = total[1].astype(BF16)


SMEM = pl.BlockSpec(memory_space=pltpu.SMEM)
VMEM = pl.BlockSpec(memory_space=pltpu.VMEM)


def call(kernel, out_shape, in_specs, out_specs, scratch=(), flops=0, moved=0, limit=40):
    return pl.pallas_call(
        kernel,
        out_shape=out_shape,
        in_specs=in_specs,
        out_specs=out_specs,
        scratch_shapes=list(scratch),
        compiler_params=pltpu.CompilerParams(vmem_limit_bytes=limit * 2**20),
        cost_estimate=pl.CostEstimate(flops=flops, bytes_accessed=moved, transcendentals=0),
    )


def ring(size, by):
    return [(i, (i + by) % size) for i in range(size)]


def local(queries, keys, values, outputs, dout, docs):
    heads, tok, width = queries.shape
    nz = lax.axis_size("z")
    scale = 1.0 / math.sqrt(width)
    factor = scale * LOG2E
    x, y, z, c = (lax.axis_index(name) for name in ("x", "y", "z", "c"))
    place = jnp.stack([x * NC + c, x, y, z, c]).astype(jnp.int32)
    share = tok // (NX * NC)
    shape = jax.ShapeDtypeStruct
    swap = ring(NC, 1)

    def shift(k, back=False):
        pairs = [(b * NX + a, (b - a) % NY * NX + (a + k) % NX) for b in range(NY) for a in range(NX)]
        return [(j, i) for i, j in pairs] if back else pairs

    sent, pieces = call(
        prep_kernel,
        (shape((2 * (tok + EXTRA), width), BF16), shape((nz, 2 * share + EXTRA, width), BF16)),
        [SMEM] + [VMEM] * 6,
        [VMEM] * 2,
        moved=2 * 2**20,
        limit=60,
    )(place, queries[0], dout[0], outputs[0], keys, values, docs.reshape(1, tok))

    skewed = lax.ppermute(sent, ("y", "x"), shift(0))
    along = lax.all_to_all(pieces, "z", 0, 0, tiled=True)
    along, skewed = lax.optimization_barrier((along, skewed))
    moved = [skewed] + [lax.ppermute(skewed, "x", ring(NX, k)) for k in (1, 2, 3)]
    before = lax.ppermute(along, "y", ring(NY, 1))
    after = lax.ppermute(along, "y", ring(NY, -1))
    far_keys = lax.ppermute(before[:, : share + EXTRA], "y", ring(NY, 1))
    far_values = lax.ppermute(after[:, share + EXTRA :], "y", ring(NY, -1))
    moved, far_keys, far_values = lax.optimization_barrier((moved, far_keys, far_values))
    own = call(stack_kernel, shape((NX,) + sent.shape, BF16), [VMEM] * NX, VMEM, moved=2**21)(
        *moved
    )
    peer = lax.ppermute(own, "c", swap)

    total = share * nz * NY
    high, ends = call(
        functools.partial(high_kernel, share, nz),
        (shape((NY, 1, tok), F32), shape((NY, 2), jnp.int32)),
        [SMEM],
        [VMEM, SMEM],
    )(place)
    lse_part, key_all, low, bounds = call(
        functools.partial(stats_kernel, factor),
        (
            shape((NC * NY, 1, tok), F32),
            shape((total, width), BF16),
            shape((NY, 1, tok), F32),
            shape((NY, 4), jnp.int32),
        ),
        [SMEM] * 2 + [VMEM] * 7,
        [VMEM] * 3 + [SMEM],
        flops=2 * 10**9,
        moved=4 * 2**20,
    )(place, ends, own, peer, high, along, before, far_keys, after)

    lse_chip = join(lse_part, lax.ppermute(lse_part, "c", swap))
    lse_all = [lse_chip] + [lax.ppermute(lse_chip, "x", ring(NX, k)) for k in (1, 3, 2)]

    dq_shape = shape((NY, tok, width), F32)
    slab_shape = shape((nz, 2, share, width), BF16)
    far_shape = shape((nz, share, width), BF16)
    dq_own, dq_peer, here, up, down, far_dk, far_dv = call(
        functools.partial(grad_kernel, factor, scale),
        (dq_shape, dq_shape, slab_shape, slab_shape, slab_shape, far_shape, far_shape),
        [SMEM] * 2 + [VMEM] * 13,
        [VMEM] * 7,
        scratch=(
            pltpu.VMEM((total, width), BF16),
            pltpu.VMEM((total, width), F32),
            pltpu.VMEM((total, width), F32),
            pltpu.VMEM((NC * NY, 1, tok), F32),
            pltpu.VMEM((NC, width, tok), F32),
        ),
        flops=8 * 10**9,
        moved=8 * 2**20,
    )(place, bounds, own, peer, high, along, before, far_values, after, key_all, low, *lse_all)

    one = shape((tok, width), BF16)
    kept, *away = call(query_kernel, (one,) * NX, [VMEM] * 2, [VMEM] * NX, moved=3 * 2**20)(
        dq_own, lax.ppermute(dq_peer, "c", swap)
    )
    got_dk = lax.ppermute(far_dk, "y", ring(NY, 1))
    got_dv = lax.ppermute(far_dv, "y", ring(NY, -1))
    up, down = call(relay_kernel, (slab_shape,) * 2, [VMEM] * 4, [VMEM] * 2, moved=5 * 2**18)(up, down, got_dk, got_dv)
    arrived = [here, lax.ppermute(up, "y", ring(NY, 1)), lax.ppermute(down, "y", ring(NY, -1))]
    away = [lax.ppermute(away[k - 1], "x", ring(NX, -k)) for k in (1, 2, 3)]
    arrived, away = lax.optimization_barrier((arrived, away))
    slab_sum = call(add_kernel, slab_shape, [VMEM] * 3, VMEM, moved=5 * 2**18)(*arrived)
    blocks = lax.all_to_all(slab_sum, "z", 0, 0, tiled=True)
    half = shape((share, width), BF16)
    dk, dv = call(last_kernel, (half, half), [VMEM], [VMEM] * 2, moved=2**18)(blocks)

    dq = call(add_kernel, one, [VMEM] * 4, VMEM, moved=2**19)(kept, *away)
    dq = lax.ppermute(dq, ("y", "x"), shift(0, True))
    return dq[None], dk, dv


def solution(mesh):
    nz = mesh.devices.shape[0] // NY
    fine = Mesh(mesh.devices.reshape(NY, nz, NX, NC), ("y", "z", "x", "c"))
    tokens, heads = ("y", "z"), ("x", "c")
    in_specs = (
        P(heads, tokens, None),
        P(tokens, None),
        P(tokens, None),
        P(heads, tokens, None),
        P(heads, tokens, None),
        P(tokens),
    )
    out_specs = (P(heads, tokens, None), P(tokens + heads, None), P(tokens + heads, None))
    return jax.shard_map(local, mesh=fine, in_specs=in_specs, out_specs=out_specs, check_vma=False)
```

```python
import functools
import math

import jax
import jax.numpy as jnp
from jax import lax
from jax.experimental import pallas as pl
from jax.experimental.pallas import tpu as pltpu
from jax.sharding import Mesh
from jax.sharding import PartitionSpec as P

BF16 = jnp.bfloat16
F32 = jnp.float32
NY, NX, NC = 4, 4, 2
DOCS = 64
EXTRA = 16
LOW = -1e30
TILE = 256
LOG2E = 1.0 / math.log(2.0)


def dot(left, right, left_dim, right_dim):
    return lax.dot_general(
        left, right, (((left_dim,), (right_dim,)), ((), ())), preferred_element_type=F32
    )


def share_index():
    return lax.axis_index("x") * NC + lax.axis_index("c")


def split_row(row, count):
    part = row.shape[1] // count
    return [row[:, i * part : (i + 1) * part] for i in range(count)]


def rows_to_line(block):
    return jnp.concatenate([block[i : i + 1] for i in range(block.shape[0])], axis=1)


def prep_kernel(q, do, out, keys, values, docs, sent, pieces):
    tok, width = q.shape
    at = tok + EXTRA
    docs_rows = jnp.concatenate(split_row(docs[...].astype(F32), tok // width), axis=0)
    sent[0:tok, :] = q[...]
    pad = jnp.zeros((EXTRA - docs_rows.shape[0], width), F32)
    sent[tok:at, :] = jnp.concatenate([docs_rows, pad], axis=0).astype(BF16)
    prod = do[...].astype(F32) * out[...].astype(F32)
    delta = jnp.sum(jnp.transpose(prod), axis=0, keepdims=True)
    rows = jnp.concatenate(split_row(delta, tok // width), axis=0)
    high = rows.astype(BF16).astype(F32)
    middle = (rows - high).astype(BF16).astype(F32)
    low = rows - high - middle
    pad = jnp.zeros((EXTRA - 3 * rows.shape[0], width), F32)
    sent[at : at + tok, :] = do[...]
    sent[at + tok : 2 * at, :] = jnp.concatenate([high, middle, low, pad], axis=0).astype(BF16)
    share = (pieces.shape[1] - EXTRA) // 2
    first = pl.multiple_of(share_index() * share, share)
    line = lax.broadcasted_iota(jnp.int32, docs_rows.shape, 0)
    mine = jnp.sum(jnp.where(line == share_index() // NC, docs_rows, 0.0), axis=0, keepdims=True)
    line = lax.broadcasted_iota(jnp.int32, (EXTRA, width), 0)
    extra = jnp.where(line == 0, mine, 0.0).astype(BF16)
    key_rows, value_rows = keys[pl.ds(first, share), :], values[pl.ds(first, share), :]
    for i in range(pieces.shape[0]):
        pieces[i, 0:share, :] = key_rows
        pieces[i, share : share + EXTRA, :] = extra
        pieces[i, share + EXTRA :, :] = value_rows


def high_kernel(share, nz, rows, ends):
    x, y, z = (lax.axis_index(name) for name in ("x", "y", "z"))
    tok = rows.shape[2]
    line = lax.broadcasted_iota(jnp.int32, (1, tok), 1)
    for m in range(NX):
        before, skipped = (lax.rem(y + x - m + NX, NY) * nz + z) * share, share_index() * share
        rows[m] = (before + jnp.clip(line - skipped + 1, 0, share)).astype(F32)
        ends[m, 0] = before + jnp.clip(1 - skipped, 0, share)
        ends[m, 1] = before + jnp.clip(tok - skipped, 0, share)


def tile_loops(bounds, m, share, step, carry):
    start = bounds[m, 0] // share * share
    count = (bounds[m, 3] - start) // share
    fold = TILE // share
    rest = lax.rem(count - 1, fold) + 1
    whole = (count - rest) // fold
    unclear = jnp.clip((bounds[m, 1] - start + TILE - 1) // TILE, 0, whole)

    def run(masked, size, i, carry):
        return step(masked, size, pl.multiple_of(start + i * TILE, share), carry)

    carry = lax.fori_loop(0, unclear, functools.partial(run, True, TILE), carry)
    carry = lax.fori_loop(unclear, whole, functools.partial(run, False, TILE), carry)
    small = jnp.where(2 * rest <= fold, 1, 0)
    carry = lax.fori_loop(whole, whole + small, functools.partial(run, True, TILE // 2), carry)
    return lax.fori_loop(whole, whole + 1 - small, functools.partial(run, True, TILE), carry)


def visible_of(first, size, tok, low, high):
    index = (lax.broadcasted_iota(jnp.int32, (size, tok), 0) + first).astype(F32)
    return (index >= low) & (index < high)


def stats_kernel(factor, ends, own, peer, high_in, p0, p1, p2, p3, lse, key_all, low_out, bounds):
    x, y, c = (lax.axis_index(name) for name in ("x", "y", "c"))
    nz, rows, width = p2.shape
    share = rows - EXTRA
    tok = own.shape[1] // 2 - EXTRA
    number = lax.broadcasted_iota(jnp.int32, (DOCS, width), 0).astype(F32)
    below = jnp.zeros((DOCS, width), F32)
    for k, piece in enumerate((p0, p1, p2, p3)):
        for i in range(nz):
            where = block_row(y, k, i, nz, share)
            key_all[pl.ds(where, share), :] = piece[i, 0:share, :]
            docs = piece[i, share : share + EXTRA, :].astype(F32)[0:1, :]
            below = below + jnp.where(docs < number, 1.0, 0.0)
    end = NY * nz * share
    key_all[end:, :] = jnp.zeros_like(key_all[end:, :])
    lane = lax.broadcasted_iota(jnp.int32, (DOCS, width), 1)
    ours = (lane >= c * share) & (lane < (c + 1) * share)
    below = jnp.sum(jnp.where(ours, below, 0.0), axis=1, keepdims=True)
    number = lax.broadcasted_iota(jnp.int32, (DOCS, tok), 0).astype(F32)
    for m in range(NY):
        docs = rows_to_line(own[m, tok : tok + EXTRA, :].astype(F32)[0 : tok // width])
        low = jnp.sum(jnp.where(docs == number, below, 0.0), axis=0, keepdims=True)
        low_out[m] = low
        bounds[m, 0] = jnp.min(low).astype(jnp.int32)
        bounds[m, 1] = jnp.max(low).astype(jnp.int32)
        bounds[m, 2] = ends[m, 0]
        bounds[m, 3] = ends[m, 1]

    def group(m, carry):
        low = low_out[m]
        high = high_in[m]
        pair = [sets[m, 0:tok, :] for sets in (own, peer)]

        def step(masked, size, first, state):
            key = key_all[pl.ds(first, size), :]
            visible = visible_of(first, size, tok, low, high) if masked else None
            after = []
            for query, (top, total) in zip(pair, state):
                score = dot(key, query, 1, 1) * factor
                if masked:
                    score = jnp.where(visible, score, LOW)
                for part in range(size // 64):
                    piece = score[part * 64 : (part + 1) * 64].reshape(8, 8, tok)
                    new_top = jnp.maximum(top, jnp.max(piece, axis=0))
                    terms = jnp.sum(jnp.exp2(piece - new_top[None]), axis=0)
                    top, total = new_top, total * jnp.exp2(top - new_top) + terms
                after.append((top, total))
            return tuple(after)

        start = (jnp.full((8, tok), LOW, F32), jnp.zeros((8, tok), F32))
        for half, (top, total) in enumerate(tile_loops(bounds, m, share, step, (start,) * NC)):
            tops, top = top, jnp.max(top, axis=0, keepdims=True)
            total = jnp.sum(total * jnp.exp2(tops - top), axis=0, keepdims=True)
            lse[NC * lax.rem(x - m + NX, NX) + (NC - 1 - c if half else c)] = jnp.where(top > LOW, top + jnp.log2(jnp.maximum(total, 1e-30)), LOW)
        return carry

    lax.fori_loop(0, NY, group, 0)


def join(*parts):
    top = functools.reduce(jnp.maximum, parts)
    return top + jnp.log2(sum(jnp.exp2(part - top) for part in parts))


def grad_kernel(
    factor, scale, bounds, own, peer, high_in, p0, p1, p2, p3, key_all, low_in, l0, l1, l2, l3,
    dq_own, dq_peer, here, up, down, far_dk, far_dv, value_all, dk, dv, lse, dq_turned,
):
    x, y, c = (lax.axis_index(name) for name in ("x", "y", "c"))
    nz, share, width = p2.shape
    slab = nz * share
    tok = own.shape[1] // 2 - EXTRA
    for k, piece in enumerate((p0, p1, p2, p3)):
        for i in range(nz):
            where = block_row(y, k, i, nz, share)
            value_all[pl.ds(where, share), :] = piece[i, piece.shape[1] - share :, :]
    value_all[NY * slab :, :] = jnp.zeros_like(value_all[NY * slab :, :])
    dk[...] = jnp.zeros_like(dk)
    dv[...] = jnp.zeros_like(dv)
    lse[...] = join(l0[...], l1[...], l2[...], l3[...])
    n = tok // width

    def group(m, carry):
        low = low_in[m]
        high = high_in[m]
        heads = []
        for sets, head in ((own, c), (peer, NC - 1 - c)):
            at = tok + EXTRA
            extra = sets[m, at + tok : 2 * at, :].astype(F32)
            delta = rows_to_line(extra[0:n] + extra[n : 2 * n] + extra[2 * n : 3 * n])
            heads.append((sets[m, 0:tok, :], sets[m, at : at + tok, :], delta, lse[NC * lax.rem(x - m + NX, NX) + head]))
        dq_turned[...] = jnp.zeros_like(dq_turned)

        def step(masked, size, first, carry):
            at = pl.ds(first, size)
            key, value = key_all[at, :], value_all[at, :]
            visible = visible_of(first, size, tok, low, high) if masked else None
            new_dk, new_dv = dk[at, :], dv[at, :]
            scores = [dot(key, head[0], 1, 1) for head in heads]
            dprobs = [dot(value, head[1], 1, 1) for head in heads]
            for half, (query, grad, delta, norm) in enumerate(heads):
                prob = jnp.exp2(scores[half] * factor - norm)
                if masked:
                    prob = jnp.where(visible, prob, 0.0)
                dscore = (prob * (dprobs[half] - delta)).astype(BF16)
                new_dv = new_dv + dot(prob.astype(BF16), grad, 1, 0)
                new_dk = new_dk + dot(dscore, query, 1, 0)
                dq_turned[half] += dot(key, dscore, 0, 0)
            dk[at, :] = new_dk
            dv[at, :] = new_dv
            return carry

        tile_loops(bounds, m, share, step, 0)
        dq_own[m] = dq_turned[0] * scale
        dq_peer[m] = (dq_turned[1] * scale).astype(BF16)
        return carry

    lax.fori_loop(0, NY, group, 0)

    def slab_of(ref, by):
        at = pl.ds(pl.multiple_of(lax.rem(y + by, NY) * slab, slab), slab)
        return (ref[at, :] * (scale if ref is dk else 1.0)).astype(BF16).reshape(nz, share, width)

    for out, by in ((here, 0), (up, 1), (down, NY - 1)):
        out[:, 0] = slab_of(dk, by)
        out[:, 1] = slab_of(dv, by)
    far_dk[...] = slab_of(dk, 2)
    far_dv[...] = slab_of(dv, 2)


def block_row(y, k, i, nz, share):
    return pl.multiple_of((lax.rem(y - k + NY, NY) * nz + i) * share, share)


def query_kernel(own, there, *outs):
    for k, out in enumerate(outs):
        out[...] = (own[k] + there[k].astype(F32)).astype(BF16)


def stack_kernel(*refs):
    for i, piece in enumerate(refs[:-1]):
        refs[-1][i] = piece[...]


def add_kernel(*refs):
    total = refs[0][...].astype(F32)
    for ref in refs[1:-1]:
        total = total + ref[...].astype(F32)
    refs[-1][...] = total.astype(BF16)


def turn_kernel(part, out):
    out[...] = jnp.transpose(part[...].astype(F32)).astype(BF16)


def relay_kernel(up, down, got_dk, got_dv, new_up, new_down):
    new_up[:, 0] = (up[:, 0].astype(F32) + got_dk[...].astype(F32)).astype(BF16)
    new_up[:, 1] = up[:, 1]
    new_down[:, 0] = down[:, 0]
    new_down[:, 1] = (down[:, 1].astype(F32) + got_dv[...].astype(F32)).astype(BF16)


def last_kernel(blocks, dk, dv):
    total = blocks[0].astype(F32)
    for i in range(1, blocks.shape[0]):
        total = total + blocks[i].astype(F32)
    dk[...] = total[0].astype(BF16)
    dv[...] = total[1].astype(BF16)


SMEM = pl.BlockSpec(memory_space=pltpu.SMEM)
VMEM = pl.BlockSpec(memory_space=pltpu.VMEM)


def call(kernel, out_shape, in_specs, out_specs, scratch=(), flops=0, moved=0, limit=40):
    return pl.pallas_call(
        kernel,
        out_shape=out_shape,
        in_specs=in_specs,
        out_specs=out_specs,
        scratch_shapes=list(scratch),
        compiler_params=pltpu.CompilerParams(vmem_limit_bytes=limit * 2**20),
        cost_estimate=pl.CostEstimate(flops=flops, bytes_accessed=moved, transcendentals=0),
    )


def ring(size, by):
    return [(i, (i + by) % size) for i in range(size)]


def local(queries, keys, values, outputs, dout, docs):
    heads, tok, width = queries.shape
    nz = lax.axis_size("z")
    scale = 1.0 / math.sqrt(width)
    factor = scale * LOG2E
    share = tok // (NX * NC)
    shape = jax.ShapeDtypeStruct
    swap = ring(NC, 1)

    def shift(k, back=False):
        pairs = [(b * NX + a, (b - a) % NY * NX + (a + k) % NX) for b in range(NY) for a in range(NX)]
        return [(j, i) for i, j in pairs] if back else pairs

    sent, pieces = call(
        prep_kernel,
        (shape((2 * (tok + EXTRA), width), BF16), shape((nz, 2 * share + EXTRA, width), BF16)),
        [VMEM] * 6,
        [VMEM] * 2,
        moved=2 * 2**20,
        limit=60,
    )(queries[0], dout[0], outputs[0], keys, values, docs.reshape(1, tok))

    skewed = lax.ppermute(sent, ("y", "x"), shift(0))
    along = lax.all_to_all(pieces, "z", 0, 0, tiled=True)
    along, skewed = lax.optimization_barrier((along, skewed))
    moved = [skewed] + [lax.ppermute(skewed, "x", ring(NX, k)) for k in (1, 2, 3)]
    before = lax.ppermute(along, "y", ring(NY, 1))
    after = lax.ppermute(along, "y", ring(NY, -1))
    far_keys = lax.ppermute(before[:, : share + EXTRA], "y", ring(NY, 1))
    far_values = lax.ppermute(after[:, share + EXTRA :], "y", ring(NY, -1))
    moved, far_keys, far_values = lax.optimization_barrier((moved, far_keys, far_values))
    own = call(stack_kernel, shape((NX,) + sent.shape, BF16), [VMEM] * NX, VMEM, moved=2**21)(
        *moved
    )
    peer = lax.ppermute(own, "c", swap)

    total = share * nz * NY + TILE // 2
    high, ends = call(
        functools.partial(high_kernel, share, nz),
        (shape((NY, 1, tok), F32), shape((NY, 2), jnp.int32)),
        [],
        [VMEM, SMEM],
    )()
    lse_part, key_all, low, bounds = call(
        functools.partial(stats_kernel, factor),
        (
            shape((NC * NY, 1, tok), F32),
            shape((total, width), BF16),
            shape((NY, 1, tok), F32),
            shape((NY, 4), jnp.int32),
        ),
        [SMEM] + [VMEM] * 7,
        [VMEM] * 3 + [SMEM],
        flops=2 * 10**9,
        moved=4 * 2**20,
    )(ends, own, peer, high, along, before, far_keys, after)

    lse_chip = join(lse_part, lax.ppermute(lse_part, "c", swap))
    lse_all = [lse_chip] + [lax.ppermute(lse_chip, "x", ring(NX, k)) for k in (1, 3, 2)]

    dq_shape, peer_shape = (shape((NX, width, tok), kind) for kind in (F32, BF16))
    slab_shape = shape((nz, 2, share, width), BF16)
    far_shape = shape((nz, share, width), BF16)
    dq_own, dq_peer, here, up, down, far_dk, far_dv = call(
        functools.partial(grad_kernel, factor, scale),
        (dq_shape, peer_shape, slab_shape, slab_shape, slab_shape, far_shape, far_shape),
        [SMEM] + [VMEM] * 13,
        [VMEM] * 7,
        scratch=(
            pltpu.VMEM((total, width), BF16),
            pltpu.VMEM((total, width), F32),
            pltpu.VMEM((total, width), F32),
            pltpu.VMEM((NC * NY, 1, tok), F32),
            pltpu.VMEM((NC, width, tok), F32),
        ),
        flops=8 * 10**9,
        moved=8 * 2**20,
    )(bounds, own, peer, high, along, before, far_values, after, key_all, low, *lse_all)

    one = shape((width, tok), BF16)
    kept, *away = call(query_kernel, (one,) * NX, [VMEM] * 2, [VMEM] * NX, moved=3 * 2**20)(
        dq_own, lax.ppermute(dq_peer, "c", swap)
    )
    got_dk = lax.ppermute(far_dk, "y", ring(NY, 1))
    got_dv = lax.ppermute(far_dv, "y", ring(NY, -1))
    got_dk, got_dv, kept = lax.optimization_barrier((got_dk, got_dv, kept))
    up, down = call(relay_kernel, (slab_shape,) * 2, [VMEM] * 4, [VMEM] * 2, moved=5 * 2**18)(up, down, got_dk, got_dv)
    arrived = [here, lax.ppermute(up, "y", ring(NY, 1)), lax.ppermute(down, "y", ring(NY, -1))]
    away = [lax.ppermute(away[k - 1], "x", ring(NX, -k)) for k in (1, 2, 3)]
    arrived, away = lax.optimization_barrier((arrived, away))
    slab_sum = call(add_kernel, slab_shape, [VMEM] * 3, VMEM, moved=5 * 2**18)(*arrived)
    blocks = lax.all_to_all(slab_sum, "z", 0, 0, tiled=True)
    dq = call(add_kernel, one, [VMEM] * 4, VMEM, moved=2**19)(kept, *away)
    dq = lax.ppermute(dq, ("y", "x"), shift(0, True))
    dq = call(turn_kernel, shape((tok, width), BF16), [VMEM], VMEM, moved=2**18)(dq)
    blocks, dq = lax.optimization_barrier((blocks, dq))
    half = shape((share, width), BF16)
    dk, dv = call(last_kernel, (half, half), [VMEM], [VMEM] * 2, moved=2**18)(blocks)
    return dq[None], dk, dv


def solution(mesh):
    nz = mesh.devices.shape[0] // NY
    fine = Mesh(mesh.devices.reshape(NY, nz, NX, NC), ("y", "z", "x", "c"))
    tokens, heads = ("y", "z"), ("x", "c")
    in_specs = (
        P(heads, tokens, None),
        P(tokens, None),
        P(tokens, None),
        P(heads, tokens, None),
        P(heads, tokens, None),
        P(tokens),
    )
    out_specs = (P(heads, tokens, None), P(tokens + heads, None), P(tokens + heads, None))
    return jax.shard_map(local, mesh=fine, in_specs=in_specs, out_specs=out_specs, check_vma=False)
```

```python
import functools
import math

import jax
import jax.numpy as jnp
from jax import lax
from jax.experimental import pallas as pl
from jax.experimental.pallas import tpu as pltpu
from jax.sharding import Mesh
from jax.sharding import PartitionSpec as P

BF16 = jnp.bfloat16
F32 = jnp.float32
NY, NX, NC = 4, 4, 2
DOCS = 64
EXTRA = 16
LOW = -1e30
TILE = 256
LOG2E = 1.0 / math.log(2.0)


def dot(left, right, left_dim, right_dim):
    return lax.dot_general(
        left, right, (((left_dim,), (right_dim,)), ((), ())), preferred_element_type=F32
    )


def share_index():
    return lax.axis_index("x") * NC + lax.axis_index("c")


def split_row(row, count):
    part = row.shape[1] // count
    return [row[:, i * part : (i + 1) * part] for i in range(count)]


def rows_to_line(block):
    return jnp.concatenate([block[i : i + 1] for i in range(block.shape[0])], axis=1)


def prep_kernel(q, do, out, keys, values, docs, sent, pieces):
    tok, width = q.shape
    at = tok + EXTRA
    docs_rows = jnp.concatenate(split_row(docs[...].astype(F32), tok // width), axis=0)
    sent[0:tok, :] = q[...]
    pad = jnp.zeros((EXTRA - docs_rows.shape[0], width), F32)
    sent[tok:at, :] = jnp.concatenate([docs_rows, pad], axis=0).astype(BF16)
    prod = do[...].astype(F32) * out[...].astype(F32)
    delta = jnp.sum(jnp.transpose(prod), axis=0, keepdims=True)
    rows = jnp.concatenate(split_row(delta, tok // width), axis=0)
    high = rows.astype(BF16).astype(F32)
    middle = (rows - high).astype(BF16).astype(F32)
    low = rows - high - middle
    pad = jnp.zeros((EXTRA - 3 * rows.shape[0], width), F32)
    sent[at : at + tok, :] = do[...]
    sent[at + tok : 2 * at, :] = jnp.concatenate([high, middle, low, pad], axis=0).astype(BF16)
    share = (pieces.shape[1] - EXTRA) // 2
    first = pl.multiple_of(share_index() * share, share)
    line = lax.broadcasted_iota(jnp.int32, docs_rows.shape, 0)
    mine = jnp.sum(jnp.where(line == share_index() // NC, docs_rows, 0.0), axis=0, keepdims=True)
    line = lax.broadcasted_iota(jnp.int32, (EXTRA, width), 0)
    extra = jnp.where(line == 0, mine, 0.0).astype(BF16)
    key_rows, value_rows = keys[pl.ds(first, share), :], values[pl.ds(first, share), :]
    for i in range(pieces.shape[0]):
        pieces[i, 0:share, :] = key_rows
        pieces[i, share : share + EXTRA, :] = extra
        pieces[i, share + EXTRA :, :] = value_rows


def high_kernel(share, nz, rows, ends):
    x, y, z = (lax.axis_index(name) for name in ("x", "y", "z"))
    tok = rows.shape[2]
    line = lax.broadcasted_iota(jnp.int32, (1, tok), 1)
    for m in range(NX):
        before, skipped = (lax.rem(y + x - m + NX, NY) * nz + z) * share, share_index() * share
        rows[m] = (before + jnp.clip(line - skipped + 1, 0, share)).astype(F32)
        ends[m, 0] = before + jnp.clip(1 - skipped, 0, share)
        ends[m, 1] = before + jnp.clip(tok - skipped, 0, share)


def tile_loops(bounds, m, share, step, carry):
    start = bounds[m, 0] // share * share
    count = (bounds[m, 3] - start) // share
    fold = TILE // share
    rest = lax.rem(count - 1, fold) + 1
    whole = (count - rest) // fold
    unclear = jnp.clip((bounds[m, 1] - start + TILE - 1) // TILE, 0, whole)

    def run(masked, size, i, carry):
        return step(masked, size, pl.multiple_of(start + i * TILE, share), carry)

    carry = lax.fori_loop(0, unclear, functools.partial(run, True, TILE), carry)
    carry = lax.fori_loop(unclear, whole, functools.partial(run, False, TILE), carry)
    small = jnp.where(2 * rest <= fold, 1, 0)
    carry = lax.fori_loop(whole, whole + small, functools.partial(run, True, TILE // 2), carry)
    return lax.fori_loop(whole, whole + 1 - small, functools.partial(run, True, TILE), carry)


def visible_of(first, size, tok, low, high):
    index = (lax.broadcasted_iota(jnp.int32, (size, tok), 0) + first).astype(F32)
    return (index >= low) & (index < high)


def stats_kernel(factor, ends, own, peer, high_in, p0, p1, p2, p3, lse, key_all, low_out, bounds):
    x, y, c = (lax.axis_index(name) for name in ("x", "y", "c"))
    nz, rows, width = p2.shape
    share = rows - EXTRA
    tok = own.shape[1] // 2 - EXTRA
    number = lax.broadcasted_iota(jnp.int32, (DOCS, width), 0).astype(F32)
    below = jnp.zeros((DOCS, width), F32)
    for k, piece in enumerate((p0, p1, p2, p3)):
        for i in range(nz):
            where = block_row(y, k, i, nz, share)
            key_all[pl.ds(where, share), :] = piece[i, 0:share, :]
            docs = piece[i, share : share + EXTRA, :].astype(F32)[0:1, :]
            below = below + jnp.where(docs < number, 1.0, 0.0)
    end = NY * nz * share
    key_all[end:, :] = jnp.zeros_like(key_all[end:, :])
    lane = lax.broadcasted_iota(jnp.int32, (DOCS, width), 1)
    ours = (lane >= c * share) & (lane < (c + 1) * share)
    below = jnp.sum(jnp.where(ours, below, 0.0), axis=1, keepdims=True)
    number = lax.broadcasted_iota(jnp.int32, (DOCS, tok), 0).astype(F32)
    for m in range(NY):
        docs = rows_to_line(own[m, tok : tok + EXTRA, :].astype(F32)[0 : tok // width])
        low = jnp.sum(jnp.where(docs == number, below, 0.0), axis=0, keepdims=True)
        low_out[m] = low
        bounds[m, 0] = jnp.min(low).astype(jnp.int32)
        bounds[m, 1] = jnp.max(low).astype(jnp.int32)
        bounds[m, 2] = ends[m, 0]
        bounds[m, 3] = ends[m, 1]

    def group(m, carry):
        low = low_out[m]
        high = high_in[m]
        pair = [sets[m, 0:tok, :] for sets in (own, peer)]

        def step(masked, size, first, state):
            key = key_all[pl.ds(first, size), :]
            visible = visible_of(first, size, tok, low, high) if masked else None
            after = []
            for query, (top, total) in zip(pair, state):
                score = dot(key, query, 1, 1) * factor
                if masked:
                    score = jnp.where(visible, score, LOW)
                for part in range(size // 64):
                    piece = score[part * 64 : (part + 1) * 64].reshape(8, 8, tok)
                    new_top = jnp.maximum(top, jnp.max(piece, axis=0))
                    terms = jnp.sum(jnp.exp2(piece - new_top[None]), axis=0)
                    top, total = new_top, total * jnp.exp2(top - new_top) + terms
                after.append((top, total))
            return tuple(after)

        start = (jnp.full((8, tok), LOW, F32), jnp.zeros((8, tok), F32))
        for half, (top, total) in enumerate(tile_loops(bounds, m, share, step, (start,) * NC)):
            tops, top = top, jnp.max(top, axis=0, keepdims=True)
            total = jnp.sum(total * jnp.exp2(tops - top), axis=0, keepdims=True)
            lse[NC * lax.rem(x - m + NX, NX) + (NC - 1 - c if half else c)] = jnp.where(top > LOW, top + jnp.log2(jnp.maximum(total, 1e-30)), LOW)
        return carry

    lax.fori_loop(0, NY, group, 0)


def join(*parts):
    top = functools.reduce(jnp.maximum, parts)
    return top + jnp.log2(sum(jnp.exp2(part - top) for part in parts))


def grad_kernel(
    factor, scale, bounds, own, peer, high_in, p0, p1, p2, p3, key_all, low_in, l0, l1, l2, l3,
    dq_own, dq_peer, here, up, down, far_dk, far_dv, value_all, dk, dv, lse, dq_turned,
):
    x, y, c = (lax.axis_index(name) for name in ("x", "y", "c"))
    nz, share, width = p2.shape
    slab = nz * share
    tok = own.shape[1] // 2 - EXTRA
    for k, piece in enumerate((p0, p1, p2, p3)):
        for i in range(nz):
            where = block_row(y, k, i, nz, share)
            value_all[pl.ds(where, share), :] = piece[i, piece.shape[1] - share :, :]
    value_all[NY * slab :, :] = jnp.zeros_like(value_all[NY * slab :, :])
    dk[...] = jnp.zeros_like(dk)
    dv[...] = jnp.zeros_like(dv)
    lse[...] = join(l0[...], l1[...], l2[...], l3[...])
    n = tok // width

    def group(m, carry):
        low = low_in[m]
        high = high_in[m]
        heads = []
        for sets, head in ((own, c), (peer, NC - 1 - c)):
            at = tok + EXTRA
            extra = sets[m, at + tok : 2 * at, :].astype(F32)
            delta = rows_to_line(extra[0:n] + extra[n : 2 * n] + extra[2 * n : 3 * n])
            heads.append((sets[m, 0:tok, :], sets[m, at : at + tok, :], delta, lse[NC * lax.rem(x - m + NX, NX) + head]))
        dq_turned[...] = jnp.zeros_like(dq_turned)

        def step(masked, size, first, carry):
            at = pl.ds(first, size)
            key, value = key_all[at, :], value_all[at, :]
            visible = visible_of(first, size, tok, low, high) if masked else None
            new_dk, new_dv = dk[at, :], dv[at, :]
            scores = [dot(key, head[0], 1, 1) for head in heads]
            dprobs = [dot(value, head[1], 1, 1) for head in heads]
            for half, (query, grad, delta, norm) in enumerate(heads):
                prob = jnp.exp2(scores[half] * factor - norm)
                if masked:
                    prob = jnp.where(visible, prob, 0.0)
                dscore = (prob * (dprobs[half] - delta)).astype(BF16)
                new_dv = new_dv + dot(prob.astype(BF16), grad, 1, 0)
                new_dk = new_dk + dot(dscore, query, 1, 0)
                dq_turned[half] += dot(key, dscore, 0, 0)
            dk[at, :] = new_dk
            dv[at, :] = new_dv
            return carry

        tile_loops(bounds, m, share, step, 0)
        dq_own[m] = dq_turned[0] * scale
        dq_peer[m] = (dq_turned[1] * scale).astype(BF16)
        return carry

    lax.fori_loop(0, NY, group, 0)

    def slab_of(ref, by):
        at = pl.ds(pl.multiple_of(lax.rem(y + by, NY) * slab, slab), slab)
        return (ref[at, :] * (scale if ref is dk else 1.0)).astype(BF16).reshape(nz, share, width)

    for out, by in ((here, 0), (up, 1), (down, NY - 1)):
        out[:, 0] = slab_of(dk, by)
        out[:, 1] = slab_of(dv, by)
    far_dk[...] = slab_of(dk, 2)
    far_dv[...] = slab_of(dv, 2)


def block_row(y, k, i, nz, share):
    return pl.multiple_of((lax.rem(y - k + NY, NY) * nz + i) * share, share)


def query_kernel(own, there, *outs):
    for k, out in enumerate(outs):
        out[...] = (own[k] + there[k].astype(F32)).astype(BF16)


def stack_kernel(*refs):
    for i, piece in enumerate(refs[:-1]):
        refs[-1][i] = piece[...]


def add_kernel(*refs):
    total = refs[0][...].astype(F32)
    for ref in refs[1:-1]:
        total = total + ref[...].astype(F32)
    refs[-1][...] = total.astype(BF16)


def turn_kernel(part, out):
    out[...] = jnp.transpose(part[...].astype(F32)).astype(BF16)


def relay_kernel(up, down, got_dk, got_dv, new_up, new_down):
    new_up[:, 0] = (up[:, 0].astype(F32) + got_dk[...].astype(F32)).astype(BF16)
    new_up[:, 1] = up[:, 1]
    new_down[:, 0] = down[:, 0]
    new_down[:, 1] = (down[:, 1].astype(F32) + got_dv[...].astype(F32)).astype(BF16)


def last_kernel(blocks, dk, dv):
    total = blocks[0].astype(F32)
    for i in range(1, blocks.shape[0]):
        total = total + blocks[i].astype(F32)
    dk[...] = total[0].astype(BF16)
    dv[...] = total[1].astype(BF16)


SMEM = pl.BlockSpec(memory_space=pltpu.SMEM)
VMEM = pl.BlockSpec(memory_space=pltpu.VMEM)


def call(kernel, out_shape, in_specs, out_specs, scratch=(), flops=0, moved=0, limit=40):
    return pl.pallas_call(
        kernel,
        out_shape=out_shape,
        in_specs=in_specs,
        out_specs=out_specs,
        scratch_shapes=list(scratch),
        compiler_params=pltpu.CompilerParams(vmem_limit_bytes=limit * 2**20),
        cost_estimate=pl.CostEstimate(flops=flops, bytes_accessed=moved, transcendentals=0),
    )


def ring(size, by):
    return [(i, (i + by) % size) for i in range(size)]


def local(queries, keys, values, outputs, dout, docs):
    heads, tok, width = queries.shape
    nz = lax.axis_size("z")
    scale = 1.0 / math.sqrt(width)
    factor = scale * LOG2E
    share = tok // (NX * NC)
    shape = jax.ShapeDtypeStruct
    swap = ring(NC, 1)

    def shift(k, back=False):
        pairs = [(b * NX + a, (b - a) % NY * NX + (a + k) % NX) for b in range(NY) for a in range(NX)]
        return [(j, i) for i, j in pairs] if back else pairs

    sent, pieces = call(
        prep_kernel,
        (shape((2 * (tok + EXTRA), width), BF16), shape((nz, 2 * share + EXTRA, width), BF16)),
        [VMEM] * 6,
        [VMEM] * 2,
        moved=2 * 2**20,
        limit=60,
    )(queries[0], dout[0], outputs[0], keys, values, docs.reshape(1, tok))

    skewed = lax.ppermute(sent, ("y", "x"), shift(0))
    along = lax.all_to_all(pieces, "z", 0, 0, tiled=True)
    moved = [skewed] + [lax.ppermute(skewed, "x", ring(NX, k)) for k in (1, 2, 3)]
    before = lax.ppermute(along, "y", ring(NY, 1))
    after = lax.ppermute(along, "y", ring(NY, -1))
    far_keys = lax.ppermute(before[:, : share + EXTRA], "y", ring(NY, 1))
    far_values = lax.ppermute(after[:, share + EXTRA :], "y", ring(NY, -1))
    moved, far_keys, far_values = lax.optimization_barrier((moved, far_keys, far_values))
    own = call(stack_kernel, shape((NX,) + sent.shape, BF16), [VMEM] * NX, VMEM, moved=2**21)(
        *moved
    )
    peer = lax.ppermute(own, "c", swap)

    total = share * nz * NY + TILE // 2
    high, ends = call(
        functools.partial(high_kernel, share, nz),
        (shape((NY, 1, tok), F32), shape((NY, 2), jnp.int32)),
        [],
        [VMEM, SMEM],
    )()
    lse_part, key_all, low, bounds = call(
        functools.partial(stats_kernel, factor),
        (
            shape((NC * NY, 1, tok), F32),
            shape((total, width), BF16),
            shape((NY, 1, tok), F32),
            shape((NY, 4), jnp.int32),
        ),
        [SMEM] + [VMEM] * 7,
        [VMEM] * 3 + [SMEM],
        flops=2 * 10**9,
        moved=4 * 2**20,
    )(ends, own, peer, high, along, before, far_keys, after)

    lse_chip = join(lse_part, lax.ppermute(lse_part, "c", swap))
    lse_all = [lse_chip] + [lax.ppermute(lse_chip, "x", ring(NX, k)) for k in (1, 3, 2)]

    dq_shape, peer_shape = (shape((NX, width, tok), kind) for kind in (F32, BF16))
    slab_shape = shape((nz, 2, share, width), BF16)
    far_shape = shape((nz, share, width), BF16)
    dq_own, dq_peer, here, up, down, far_dk, far_dv = call(
        functools.partial(grad_kernel, factor, scale),
        (dq_shape, peer_shape, slab_shape, slab_shape, slab_shape, far_shape, far_shape),
        [SMEM] + [VMEM] * 13,
        [VMEM] * 7,
        scratch=(
            pltpu.VMEM((total, width), BF16),
            pltpu.VMEM((total, width), F32),
            pltpu.VMEM((total, width), F32),
            pltpu.VMEM((NC * NY, 1, tok), F32),
            pltpu.VMEM((NC, width, tok), F32),
        ),
        flops=8 * 10**9,
        moved=8 * 2**20,
    )(bounds, own, peer, high, along, before, far_values, after, key_all, low, *lse_all)

    one = shape((width, tok), BF16)
    kept, *away = call(query_kernel, (one,) * NX, [VMEM] * 2, [VMEM] * NX, moved=3 * 2**20)(
        dq_own, lax.ppermute(dq_peer, "c", swap)
    )
    got_dk = lax.ppermute(far_dk, "y", ring(NY, 1))
    got_dv = lax.ppermute(far_dv, "y", ring(NY, -1))
    away = [lax.ppermute(away[k - 1], "x", ring(NX, -k)) for k in (1, 2, 3)]
    got_dk, got_dv, away[0] = lax.optimization_barrier((got_dk, got_dv, away[0]))
    up, down = call(relay_kernel, (slab_shape,) * 2, [VMEM] * 4, [VMEM] * 2, moved=5 * 2**18)(up, down, got_dk, got_dv)
    arrived = [here, lax.ppermute(up, "y", ring(NY, 1)), lax.ppermute(down, "y", ring(NY, -1))]
    arrived, away = lax.optimization_barrier((arrived, away))
    slab_sum = call(add_kernel, slab_shape, [VMEM] * 3, VMEM, moved=5 * 2**18)(*arrived)
    blocks = lax.all_to_all(slab_sum, "z", 0, 0, tiled=True)
    dq = call(add_kernel, one, [VMEM] * 4, VMEM, moved=2**19)(kept, *away)
    dq = lax.ppermute(dq, ("y", "x"), shift(0, True))
    dq = call(turn_kernel, shape((tok, width), BF16), [VMEM], VMEM, moved=2**18)(dq)
    blocks, dq = lax.optimization_barrier((blocks, dq))
    half = shape((share, width), BF16)
    dk, dv = call(last_kernel, (half, half), [VMEM], [VMEM] * 2, moved=2**18)(blocks)
    return dq[None], dk, dv


def solution(mesh):
    nz = mesh.devices.shape[0] // NY
    fine = Mesh(mesh.devices.reshape(NY, nz, NX, NC), ("y", "z", "x", "c"))
    tokens, heads = ("y", "z"), ("x", "c")
    in_specs = (
        P(heads, tokens, None),
        P(tokens, None),
        P(tokens, None),
        P(heads, tokens, None),
        P(heads, tokens, None),
        P(tokens),
    )
    out_specs = (P(heads, tokens, None), P(tokens + heads, None), P(tokens + heads, None))
    return jax.shard_map(local, mesh=fine, in_specs=in_specs, out_specs=out_specs, check_vma=False)
```

```python
import functools
import math

import jax
import jax.numpy as jnp
from jax import lax
from jax.experimental import pallas as pl
from jax.experimental.pallas import tpu as pltpu
from jax.sharding import Mesh
from jax.sharding import PartitionSpec as P

BF16 = jnp.bfloat16
F32 = jnp.float32
NY, NX, NC = 4, 4, 2
DOCS = 64
EXTRA = 16
LOW = -1e30
TILE = 256
LOG2E = 1.0 / math.log(2.0)


def dot(left, right, left_dim, right_dim):
    return lax.dot_general(
        left, right, (((left_dim,), (right_dim,)), ((), ())), preferred_element_type=F32
    )


def share_index():
    return lax.axis_index("x") * NC + lax.axis_index("c")


def split_row(row, count):
    part = row.shape[1] // count
    return [row[:, i * part : (i + 1) * part] for i in range(count)]


def rows_to_line(block):
    return jnp.concatenate([block[i : i + 1] for i in range(block.shape[0])], axis=1)


def prep_kernel(q, do, out, keys, values, docs, sent, pieces):
    tok, width = q.shape
    at = tok + EXTRA
    docs_rows = jnp.concatenate(split_row(docs[...].astype(F32), tok // width), axis=0)
    sent[0:tok, :] = q[...]
    pad = jnp.zeros((EXTRA - docs_rows.shape[0], width), F32)
    sent[tok:at, :] = jnp.concatenate([docs_rows, pad], axis=0).astype(BF16)
    prod = do[...].astype(F32) * out[...].astype(F32)
    delta = jnp.sum(jnp.transpose(prod), axis=0, keepdims=True)
    rows = jnp.concatenate(split_row(delta, tok // width), axis=0)
    high = rows.astype(BF16).astype(F32)
    middle = (rows - high).astype(BF16).astype(F32)
    low = rows - high - middle
    pad = jnp.zeros((EXTRA - 3 * rows.shape[0], width), F32)
    sent[at : at + tok, :] = do[...]
    sent[at + tok : 2 * at, :] = jnp.concatenate([high, middle, low, pad], axis=0).astype(BF16)
    share = (pieces.shape[1] - EXTRA) // 2
    first = pl.multiple_of(share_index() * share, share)
    line = lax.broadcasted_iota(jnp.int32, docs_rows.shape, 0)
    mine = jnp.sum(jnp.where(line == share_index() // NC, docs_rows, 0.0), axis=0, keepdims=True)
    line = lax.broadcasted_iota(jnp.int32, (EXTRA, width), 0)
    extra = jnp.where(line == 0, mine, 0.0).astype(BF16)
    key_rows, value_rows = keys[pl.ds(first, share), :], values[pl.ds(first, share), :]
    for i in range(pieces.shape[0]):
        pieces[i, 0:share, :] = key_rows
        pieces[i, share : share + EXTRA, :] = extra
        pieces[i, share + EXTRA :, :] = value_rows


def high_kernel(share, nz, rows, ends):
    x, y, z = (lax.axis_index(name) for name in ("x", "y", "z"))
    tok = rows.shape[2]
    line = lax.broadcasted_iota(jnp.int32, (1, tok), 1)
    for m in range(NX):
        before, skipped = (lax.rem(y + x - m + NX, NY) * nz + z) * share, share_index() * share
        rows[m] = (before + jnp.clip(line - skipped + 1, 0, share)).astype(F32)
        ends[m, 0] = before + jnp.clip(1 - skipped, 0, share)
        ends[m, 1] = before + jnp.clip(tok - skipped, 0, share)


def tile_loops(bounds, m, share, step, carry):
    start = bounds[m, 0] // share * share
    count = (bounds[m, 3] - start) // share
    fold = TILE // share
    rest = lax.rem(count - 1, fold) + 1
    whole = (count - rest) // fold
    unclear = jnp.clip((bounds[m, 1] - start + TILE - 1) // TILE, 0, whole)

    def run(masked, size, i, carry):
        return step(masked, size, pl.multiple_of(start + i * TILE, share), carry)

    carry = lax.fori_loop(0, unclear, functools.partial(run, True, TILE), carry)
    carry = lax.fori_loop(unclear, whole, functools.partial(run, False, TILE), carry)
    small = jnp.where(2 * rest <= fold, 1, 0)
    carry = lax.fori_loop(whole, whole + small, functools.partial(run, True, TILE // 2), carry)
    return lax.fori_loop(whole, whole + 1 - small, functools.partial(run, True, TILE), carry)


def visible_of(first, size, tok, low, high):
    index = (lax.broadcasted_iota(jnp.int32, (size, tok), 0) + first).astype(F32)
    return (index >= low) & (index < high)


def stats_kernel(factor, ends, own, peer, high_in, p0, p1, p2, p3, lse, key_all, low_out, bounds):
    x, y, c = (lax.axis_index(name) for name in ("x", "y", "c"))
    nz, rows, width = p2.shape
    share = rows - EXTRA
    tok = own.shape[1] - EXTRA
    number = lax.broadcasted_iota(jnp.int32, (DOCS, width), 0).astype(F32)
    below = jnp.zeros((DOCS, width), F32)
    for k, piece in enumerate((p0, p1, p2, p3)):
        for i in range(nz):
            where = block_row(y, k, i, nz, share)
            key_all[pl.ds(where, share), :] = piece[i, 0:share, :]
            docs = piece[i, share : share + EXTRA, :].astype(F32)[0:1, :]
            below = below + jnp.where(docs < number, 1.0, 0.0)
    end = NY * nz * share
    key_all[end:, :] = jnp.zeros_like(key_all[end:, :])
    lane = lax.broadcasted_iota(jnp.int32, (DOCS, width), 1)
    ours = (lane >= c * share) & (lane < (c + 1) * share)
    below = jnp.sum(jnp.where(ours, below, 0.0), axis=1, keepdims=True)
    number = lax.broadcasted_iota(jnp.int32, (DOCS, tok), 0).astype(F32)
    for m in range(NY):
        docs = rows_to_line(own[m, tok : tok + EXTRA, :].astype(F32)[0 : tok // width])
        low = jnp.sum(jnp.where(docs == number, below, 0.0), axis=0, keepdims=True)
        low_out[m] = low
        bounds[m, 0] = jnp.min(low).astype(jnp.int32)
        bounds[m, 1] = jnp.max(low).astype(jnp.int32)
        bounds[m, 2] = ends[m, 0]
        bounds[m, 3] = ends[m, 1]

    def group(m, carry):
        low = low_out[m]
        high = high_in[m]
        pair = [sets[m, 0:tok, :] for sets in (own, peer)]

        def step(masked, size, first, state):
            key = key_all[pl.ds(first, size), :]
            visible = visible_of(first, size, tok, low, high) if masked else None
            after = []
            for query, (top, total) in zip(pair, state):
                score = dot(key, query, 1, 1) * factor
                if masked:
                    score = jnp.where(visible, score, LOW)
                for part in range(size // 64):
                    piece = score[part * 64 : (part + 1) * 64].reshape(8, 8, tok)
                    new_top = jnp.maximum(top, jnp.max(piece, axis=0))
                    terms = jnp.sum(jnp.exp2(piece - new_top[None]), axis=0)
                    top, total = new_top, total * jnp.exp2(top - new_top) + terms
                after.append((top, total))
            return tuple(after)

        start = (jnp.full((8, tok), LOW, F32), jnp.zeros((8, tok), F32))
        for half, (top, total) in enumerate(tile_loops(bounds, m, share, step, (start,) * NC)):
            tops, top = top, jnp.max(top, axis=0, keepdims=True)
            total = jnp.sum(total * jnp.exp2(tops - top), axis=0, keepdims=True)
            lse[NC * lax.rem(x - m + NX, NX) + (NC - 1 - c if half else c)] = jnp.where(top > LOW, top + jnp.log2(jnp.maximum(total, 1e-30)), LOW)
        return carry

    lax.fori_loop(0, NY, group, 0)


def join(*parts):
    top = functools.reduce(jnp.maximum, parts)
    return top + jnp.log2(sum(jnp.exp2(part - top) for part in parts))


def grad_kernel(
    factor, scale, bounds, own, peer, grad_own, grad_peer, high_in, p0, p1, p2, p3, key_all, low_in, l0, l1, l2, l3,
    dq_own, dq_peer, here, up_dk, up_dv, down_dk, down_dv, far_dk, far_dv, value_all, dk, dv, lse, dq_turned,
):
    x, y, c = (lax.axis_index(name) for name in ("x", "y", "c"))
    nz, share, width = p2.shape
    slab = nz * share
    tok = own.shape[1] - EXTRA
    for k, piece in enumerate((p0, p1, p2, p3)):
        for i in range(nz):
            where = block_row(y, k, i, nz, share)
            value_all[pl.ds(where, share), :] = piece[i, piece.shape[1] - share :, :]
    value_all[NY * slab :, :] = jnp.zeros_like(value_all[NY * slab :, :])
    dk[...] = jnp.zeros_like(dk)
    dv[...] = jnp.zeros_like(dv)
    lse[...] = join(l0[...], l1[...], l2[...], l3[...])
    n = tok // width

    def group(m, carry):
        low = low_in[m]
        high = high_in[m]
        heads = []
        for queries, grads, head in ((own, grad_own, c), (peer, grad_peer, NC - 1 - c)):
            extra = grads[m, tok : tok + EXTRA, :].astype(F32)
            delta = rows_to_line(extra[0:n] + extra[n : 2 * n] + extra[2 * n : 3 * n])
            norm = lse[NC * lax.rem(x - m + NX, NX) + head]
            heads.append((queries[m, 0:tok, :], grads[m, 0:tok, :], delta, norm))
        dq_turned[...] = jnp.zeros_like(dq_turned)

        def step(masked, size, first, carry):
            at = pl.ds(first, size)
            key, value = key_all[at, :], value_all[at, :]
            visible = visible_of(first, size, tok, low, high) if masked else None
            new_dk, new_dv = dk[at, :], dv[at, :]
            scores = [dot(key, head[0], 1, 1) for head in heads]
            dprobs = [dot(value, head[1], 1, 1) for head in heads]
            for half, (query, grad, delta, norm) in enumerate(heads):
                prob = jnp.exp2(scores[half] * factor - norm)
                if masked:
                    prob = jnp.where(visible, prob, 0.0)
                dscore = (prob * (dprobs[half] - delta)).astype(BF16)
                new_dv = new_dv + dot(prob.astype(BF16), grad, 1, 0)
                new_dk = new_dk + dot(dscore, query, 1, 0)
                dq_turned[half] += dot(key, dscore, 0, 0)
            dk[at, :] = new_dk
            dv[at, :] = new_dv
            return carry

        tile_loops(bounds, m, share, step, 0)
        dq_own[m] = dq_turned[0] * scale
        dq_peer[m] = (dq_turned[1] * scale).astype(BF16)
        return carry

    lax.fori_loop(0, NY, group, 0)

    def slab_of(ref, by):
        at = pl.ds(pl.multiple_of(lax.rem(y + by, NY) * slab, slab), slab)
        return (ref[at, :] * (scale if ref is dk else 1.0)).astype(BF16).reshape(nz, share, width)

    here[:, 0] = slab_of(dk, 0)
    here[:, 1] = slab_of(dv, 0)
    for out_dk, out_dv, by in ((up_dk, up_dv, 1), (down_dk, down_dv, NY - 1), (far_dk, far_dv, 2)):
        out_dk[...] = slab_of(dk, by)
        out_dv[...] = slab_of(dv, by)


def block_row(y, k, i, nz, share):
    return pl.multiple_of((lax.rem(y - k + NY, NY) * nz + i) * share, share)


def query_kernel(own, there, *outs):
    for k, out in enumerate(outs):
        out[...] = (own[k] + there[k].astype(F32)).astype(BF16)


def stack_kernel(*refs):
    *pieces, queries, grads = refs
    half = queries.shape[1]
    for i, piece in enumerate(pieces):
        queries[i] = piece[0:half, :]
        grads[i] = piece[half : 2 * half, :]


def add_kernel(*refs):
    total = refs[0][...].astype(F32)
    for ref in refs[1:-1]:
        total = total + ref[...].astype(F32)
    refs[-1][...] = total.astype(BF16)


def turn_kernel(part, out):
    out[...] = jnp.transpose(part[...].astype(F32)).astype(BF16)


def slab_kernel(here, below_dk, below_dv, above_dk, above_dv, out):
    for i, parts in enumerate(((below_dk, above_dk), (below_dv, above_dv))):
        out[:, i] = (here[:, i].astype(F32) + parts[0][...].astype(F32) + parts[1][...].astype(F32)).astype(BF16)


def last_kernel(blocks, dk, dv):
    total = blocks[0].astype(F32)
    for i in range(1, blocks.shape[0]):
        total = total + blocks[i].astype(F32)
    dk[...] = total[0].astype(BF16)
    dv[...] = total[1].astype(BF16)


SMEM = pl.BlockSpec(memory_space=pltpu.SMEM)
VMEM = pl.BlockSpec(memory_space=pltpu.VMEM)


def call(kernel, out_shape, in_specs, out_specs, scratch=(), flops=0, moved=0, limit=40):
    return pl.pallas_call(
        kernel,
        out_shape=out_shape,
        in_specs=in_specs,
        out_specs=out_specs,
        scratch_shapes=list(scratch),
        compiler_params=pltpu.CompilerParams(vmem_limit_bytes=limit * 2**20),
        cost_estimate=pl.CostEstimate(flops=flops, bytes_accessed=moved, transcendentals=0),
    )


def ring(size, by):
    return [(i, (i + by) % size) for i in range(size)]


def local(queries, keys, values, outputs, dout, docs):
    heads, tok, width = queries.shape
    nz = lax.axis_size("z")
    scale = 1.0 / math.sqrt(width)
    factor = scale * LOG2E
    share = tok // (NX * NC)
    shape = jax.ShapeDtypeStruct
    swap = ring(NC, 1)

    def shift(k, back=False):
        pairs = [(b * NX + a, (b - a) % NY * NX + (a + k) % NX) for b in range(NY) for a in range(NX)]
        return [(j, i) for i, j in pairs] if back else pairs

    sent, pieces = call(
        prep_kernel,
        (shape((2 * (tok + EXTRA), width), BF16), shape((nz, 2 * share + EXTRA, width), BF16)),
        [VMEM] * 6,
        [VMEM] * 2,
        moved=2 * 2**20,
        limit=60,
    )(queries[0], dout[0], outputs[0], keys, values, docs.reshape(1, tok))

    skewed = lax.ppermute(sent, ("y", "x"), shift(0))
    along = lax.all_to_all(pieces, "z", 0, 0, tiled=True)
    moved = [skewed] + [lax.ppermute(skewed, "x", ring(NX, k)) for k in (1, 2, 3)]
    before = lax.ppermute(along, "y", ring(NY, 1))
    after = lax.ppermute(along, "y", ring(NY, -1))
    far_keys = lax.ppermute(before[:, : share + EXTRA], "y", ring(NY, 1))
    far_values = lax.ppermute(after[:, share + EXTRA :], "y", ring(NY, -1))
    moved, far_keys, far_values = lax.optimization_barrier((moved, far_keys, far_values))
    half_shape = shape((NX, tok + EXTRA, width), BF16)
    own, grad_own = call(stack_kernel, (half_shape, half_shape), [VMEM] * NX, [VMEM] * 2, moved=2**21)(*moved)
    peer = lax.ppermute(own, "c", swap)
    grad_peer = lax.ppermute(grad_own, "c", swap)

    total = share * nz * NY + TILE // 2
    high, ends = call(
        functools.partial(high_kernel, share, nz),
        (shape((NY, 1, tok), F32), shape((NY, 2), jnp.int32)),
        [],
        [VMEM, SMEM],
    )()
    lse_part, key_all, low, bounds = call(
        functools.partial(stats_kernel, factor),
        (
            shape((NC * NY, 1, tok), F32),
            shape((total, width), BF16),
            shape((NY, 1, tok), F32),
            shape((NY, 4), jnp.int32),
        ),
        [SMEM] + [VMEM] * 7,
        [VMEM] * 3 + [SMEM],
        flops=2 * 10**9,
        moved=4 * 2**20,
    )(ends, own, peer, high, along, before, far_keys, after)

    lse_chip = join(lse_part, lax.ppermute(lse_part, "c", swap))
    lse_all = [lse_chip] + [lax.ppermute(lse_chip, "x", ring(NX, k)) for k in (1, 3, 2)]

    dq_shape, peer_shape = (shape((NX, width, tok), kind) for kind in (F32, BF16))
    slab_shape = shape((nz, 2, share, width), BF16)
    far_shape = shape((nz, share, width), BF16)
    dq_own, dq_peer, here, up_dk, up_dv, down_dk, down_dv, far_dk, far_dv = call(
        functools.partial(grad_kernel, factor, scale),
        (dq_shape, peer_shape, slab_shape) + (far_shape,) * 6,
        [SMEM] + [VMEM] * 15,
        [VMEM] * 9,
        scratch=(
            pltpu.VMEM((total, width), BF16),
            pltpu.VMEM((total, width), F32),
            pltpu.VMEM((total, width), F32),
            pltpu.VMEM((NC * NY, 1, tok), F32),
            pltpu.VMEM((NC, width, tok), F32),
        ),
        flops=8 * 10**9,
        moved=8 * 2**20,
    )(bounds, own, peer, grad_own, grad_peer, high, along, before, far_values, after, key_all, low, *lse_all)

    one = shape((width, tok), BF16)
    kept, *away = call(query_kernel, (one,) * NX, [VMEM] * 2, [VMEM] * NX, moved=3 * 2**20)(
        dq_own, lax.ppermute(dq_peer, "c", swap)
    )
    got_dk = lax.ppermute(far_dk, "y", ring(NY, 1))
    got_dv = lax.ppermute(far_dv, "y", ring(NY, -1))
    away = [lax.ppermute(away[k - 1], "x", ring(NX, -k)) for k in (1, 2, 3)]
    got_dk, got_dv, kept = lax.optimization_barrier((got_dk, got_dv, kept))
    up_dk = call(add_kernel, far_shape, [VMEM] * 2, VMEM, moved=2**19)(up_dk, got_dk)
    down_dv = call(add_kernel, far_shape, [VMEM] * 2, VMEM, moved=2**19)(down_dv, got_dv)
    arrived = [here] + [lax.ppermute(part, "y", ring(NY, by)) for part, by in ((up_dk, 1), (up_dv, 1), (down_dk, -1), (down_dv, -1))]
    arrived, away = lax.optimization_barrier((arrived, away))
    slab_sum = call(slab_kernel, slab_shape, [VMEM] * 5, VMEM, moved=5 * 2**18)(*arrived)
    blocks = lax.all_to_all(slab_sum, "z", 0, 0, tiled=True)
    dq = call(add_kernel, one, [VMEM] * 4, VMEM, moved=2**19)(kept, *away)
    dq = lax.ppermute(dq, ("y", "x"), shift(0, True))
    dq = call(turn_kernel, shape((tok, width), BF16), [VMEM], VMEM, moved=2**18)(dq)
    blocks, dq = lax.optimization_barrier((blocks, dq))
    half = shape((share, width), BF16)
    dk, dv = call(last_kernel, (half, half), [VMEM], [VMEM] * 2, moved=2**18)(blocks)
    return dq[None], dk, dv


def solution(mesh):
    nz = mesh.devices.shape[0] // NY
    fine = Mesh(mesh.devices.reshape(NY, nz, NX, NC), ("y", "z", "x", "c"))
    tokens, heads = ("y", "z"), ("x", "c")
    in_specs = (
        P(heads, tokens, None),
        P(tokens, None),
        P(tokens, None),
        P(heads, tokens, None),
        P(heads, tokens, None),
        P(tokens),
    )
    out_specs = (P(heads, tokens, None), P(tokens + heads, None), P(tokens + heads, None))
    return jax.shard_map(local, mesh=fine, in_specs=in_specs, out_specs=out_specs, check_vma=False)
```
